32 devices in a mesh: gx: 8 (over z, x), gy: 4 (over y, core).
Axes of the slice: x: 2, y: 2, z: 4, core: 2. Of those that a mesh axis runs over, the one named last changes fastest.
Arguments:
- hydro: float32 [192, 192, 792], P('gx', 'gy'), may hold values from 0.05 to 2
- winds: float32 [192, 192, 24], P('gx', 'gy'), may hold values from -0.3 to 0.3
- cloud_mask: int32 [192, 192], P('gx', 'gy'), may hold values from 0 to 1, as said below
- coal_kernel: bfloat16 [4356, 66], replicated, may hold values from -0.09375 to 0.09375
- block_mask: int32 [6, 6], replicated, may hold values 0 or 1
Outputs:
- hydro_next: float32 [192, 192, 792], P('gx', 'gy')
The draws below stay inside these ranges and needn't reach their ends.
Inputs may be any that keep to these rules, and one draw needn't show every extreme that they name: `cloud_mask`: exactly 4608 columns are cloudy; the columns of one aligned tile of 24 x 48 are all cloudy.
All inputs are finite; a program needn't handle non-finite values.
Results may differ from the reference program's by a relative error of at most 0.0017.
Values may be sent and summed in bfloat16 or wider, within the bound.
A program may use at most 128 MiB of HBM per device.

```python
import math
import jax
import jax.numpy as jnp
from jax import lax

BLK = 11
CX = 24
CY = 48
LEV = 12
CH = 66
NB = 6
NX = 192
NY = 192
OWN = 144
CLOUDY = 4608


def draw_cloud_mask(key, part):
    key_bias, key_full, key_noise = jax.random.split(jax.random.fold_in(key, 11), 3)
    tiles_x = NX // CX
    tiles_y = NY // CY
    ntiles = tiles_x * tiles_y
    bias = jax.random.randint(key_bias, (ntiles,), 0, 4)
    chosen = jax.random.randint(key_full, (), 0, ntiles)
    bias = jnp.where(jnp.arange(ntiles) == chosen, 4, bias)
    tile_of = (jnp.arange(NX) // CX)[:, None] * tiles_y + (jnp.arange(NY) // CY)[None, :]
    noise = jax.random.randint(key_noise, (NX, NY), 0, 2 ** 20)
    score = bias[tile_of] * 2 ** 20 + noise
    order = jnp.argsort(-score.reshape(-1), stable=True)
    flat = jnp.zeros((NX * NY,), jnp.int32).at[order[:CLOUDY]].set(1)
    return flat.reshape(NX, NY)


def with_ends(drawn, stream_key, smallest, top_value):
    spot = [jax.random.randint(jax.random.fold_in(stream_key, axis), (), 0, length) for axis, length in enumerate(drawn.shape)]
    longest = drawn.shape.index(max(drawn.shape))
    next_to = spot[:longest] + [(spot[longest] + 1) % drawn.shape[longest]] + spot[longest + 1:]
    return drawn.at[tuple(spot)].set(smallest).at[tuple(next_to)].set(top_value)


def block_scale(stream_key, extent, pieces, low, high):
    gain = 1.0
    for position, parts in pieces:
        heights = jax.random.uniform(jax.random.fold_in(jax.random.fold_in(stream_key, 6), position), (parts,), jnp.float32, low / len(pieces), high / len(pieces))
        gain = gain * jnp.repeat(jnp.exp(heights), extent[position] // parts).reshape((-1,) + (1,) * (len(extent) - 1 - position))
    return gain


def bell_draw(stream_key, shape, spread, most, dtype=jnp.bfloat16):
    drawn = spread * jax.random.normal(stream_key, shape, jnp.float32)
    return jnp.clip(drawn, min=-most, max=most).astype(dtype)


def setup_inputs(seed: int = 0) -> dict:
    streams_of = jax.random.split(jax.random.key(seed), 6)
    return {
        "hydro": jnp.clip(jnp.exp(math.log(2.0) - 3.6888794 * jax.random.uniform(streams_of[0], (NX, NY, LEV * CH), jnp.float32) ** block_scale(streams_of[0], (NX, NY, LEV * CH), ((0, 8), (1, 4)), -0.2, 0.2)), 0.05, 2.0),
        "winds": jnp.clip(jax.random.uniform(streams_of[1], (NX, NY, 2 * LEV), jnp.float32, -0.3, 0.3) * block_scale(streams_of[1], (NX, NY, 2 * LEV), ((0, 8), (1, 4)), -0.4, 0.0), -0.3, 0.3),
        "cloud_mask": draw_cloud_mask(jax.random.fold_in(streams_of[5], 71), 0),
        "coal_kernel": bell_draw(streams_of[3], (CH * CH, CH), (CH * CH) ** -0.5, 0.09375),
        "block_mask": with_ends((jax.random.randint(streams_of[4], (NB, NB), 0, 3) < 2).astype(jnp.int32), jax.random.fold_in(streams_of[4], 1), 0, 1),
    }


def advect(hydro, winds):
    q = hydro.reshape(NX, NY, LEV, CH)
    u = winds[:, :, :LEV]
    v = winds[:, :, LEV:]

    def divergence(field, courant, axis):
        face = 0.5 * (jnp.roll(courant, 1, axis) + courant)
        flux = jnp.maximum(face, 0.0)[..., None] * jnp.roll(field, 1, axis) + jnp.minimum(face, 0.0)[..., None] * field
        return jnp.roll(flux, -1, axis) - flux

    return q - divergence(q, u, 0) - divergence(q, v, 1)


def reference(hydro, winds, cloud_mask, coal_kernel, block_mask):
    q_adv = advect(hydro, winds)
    cols = q_adv.reshape(NX * NY, LEV, CH)
    blocks_of_bin = jnp.arange(CH) // BLK
    blockmap = block_mask[blocks_of_bin[:, None], blocks_of_bin[None, :]].reshape(CH * CH, 1)
    kernel_eff = jnp.where(blockmap > 0, coal_kernel, jnp.zeros_like(coal_kernel)).astype(jnp.float32)
    index = jnp.nonzero(cloud_mask.reshape(-1), size=CLOUDY)[0].astype(jnp.int32)
    chosen = lax.optimization_barrier(cols[index].astype(jnp.bfloat16)).astype(jnp.float32)

    def block_work(block):
        cells = block.reshape(-1, CH)
        pairs = (cells[:, :, None] * cells[:, None, :]).astype(jnp.bfloat16)
        pairs = lax.optimization_barrier(pairs).astype(jnp.float32).reshape(-1, CH * CH)
        tend = jnp.dot(pairs, kernel_eff, precision=lax.Precision.HIGHEST, preferred_element_type=jnp.float32)
        tend = lax.optimization_barrier(tend.astype(jnp.bfloat16)).astype(jnp.float32)
        return tend.reshape(OWN, LEV, CH)

    tendency = lax.map(block_work, chosen.reshape(CLOUDY // OWN, OWN, LEV, CH)).reshape(CLOUDY, LEV, CH)
    result = cols.at[index].add(tendency)
    return result.reshape(NX, NY, LEV * CH)
```

```python
import jax
import jax.numpy as jnp
from jax import lax
from jax.experimental import pallas as pl
from jax.experimental.pallas import tpu as pltpu
from jax.sharding import PartitionSpec as P

BLK = 11
ROWS = 16
LANES = 128
DEPTH = 256


def round_up(value, unit):
    return (value + unit - 1) // unit * unit


def edges(array, axis, dim):
    count, length = lax.axis_size(axis), array.shape[dim]
    up = [(i, (i + 1) % count) for i in range(count)]
    down = [(j, i) for i, j in up]
    last = lax.index_in_dim(array, length - 1, dim, keepdims=False)
    first = lax.index_in_dim(array, 0, dim, keepdims=False)
    return last, first, up, down


def folded_kernel(coal_kernel, block_mask, chan):
    of_bin = jnp.repeat(jnp.repeat(block_mask, BLK, axis=0), BLK, axis=1)
    cube = coal_kernel.astype(jnp.float32).T.reshape(chan, chan, chan)
    cube = jnp.where(of_bin[None] > 0, cube, 0.0)
    both = cube + cube.transpose(0, 2, 1)
    whole = chan // ROWS * ROWS
    at = jnp.arange(chan)
    same = (at[:, None] // ROWS == at[None, :] // ROWS)[None]
    used = jnp.where(same, cube, both).astype(jnp.bfloat16)
    parts = []
    for first in range(0, whole, ROWS):
        piece = used[:, first : first + ROWS, first:whole]
        parts.append(piece.reshape(chan, -1))
    if whole < chan:
        parts.append(used[:, whole:, :whole].reshape(chan, -1))
        corner = jnp.pad(used[:, whole:, whole:], ((0, 0), (0, 0), (0, ROWS - (chan - whole))))
        parts.append(corner.reshape(chan, -1))
    flat = jnp.concatenate(parts, axis=1)
    return jnp.pad(flat, ((0, round_up(chan, ROWS) - chan), (0, round_up(flat.shape[1], DEPTH) - flat.shape[1])))


def pair_blocks(chan):
    whole = chan // ROWS * ROWS
    runs = [(i, j) for i in range(whole) for j in range(i // ROWS * ROWS, whole, ROWS)]
    runs += [(i, j) for i in range(whole, chan) for j in range(0, whole, ROWS)]
    runs += [(i, whole) for i in range(whole, chan)]
    return runs


def three_parts(value):
    high = value.astype(jnp.bfloat16)
    rest = value - high.astype(jnp.float32)
    middle = rest.astype(jnp.bfloat16)
    low = (rest - middle.astype(jnp.float32)).astype(jnp.bfloat16)
    return jnp.concatenate([high, middle, low], axis=1)


def step_kernel(levels, chan, q_ref, w_ref, left_ref, right_ref, below_ref, above_ref, mask_ref, spread_ref, fold_ref,
                out_ref, turned_ref, back_ref, flux_ref, tall_ref, wtall_ref):
    size_x, size_y, width = q_ref.shape
    top = 8

    def spread(face):
        return jnp.dot(three_parts(face), spread_ref[...], preferred_element_type=jnp.float32)

    def upwind(face, before, after):
        return jnp.maximum(face, 0.0) * before + jnp.minimum(face, 0.0) * after

    u_first = w_ref[0][:, :levels]
    face = spread(0.5 * (left_ref[:, width : width + levels] + u_first))
    flux_ref[...] = upwind(face, left_ref[:, :width], q_ref[0])

    def advect(x, q_next, u_next):
        here = q_ref[x]
        winds = w_ref[x]
        tall_ref[top : top + size_y] = here
        tall_ref[top - 1 : top] = below_ref[x][:, :width]
        tall_ref[top + size_y : top + size_y + 1] = above_ref[x][:, :width]
        wtall_ref[top : top + size_y] = winds
        wtall_ref[top - 1 : top] = below_ref[x][:, width:]
        wtall_ref[top + size_y : top + size_y + 1] = above_ref[x][:, width:]
        v = winds[:, levels:]
        v_before = wtall_ref[top - 1 : top - 1 + size_y][:, levels:]
        v_after = wtall_ref[top + 1 : top + 1 + size_y][:, levels:]
        faces = jnp.concatenate(
            [0.5 * (winds[:, :levels] + u_next), 0.5 * (v_before + v), 0.5 * (v + v_after)], axis=0
        )
        wide = spread(faces)
        flux_next = upwind(wide[:size_y], here, q_next)
        g_here = upwind(wide[size_y : 2 * size_y], tall_ref[top - 1 : top - 1 + size_y], here)
        g_next = upwind(wide[2 * size_y :], here, tall_ref[top + 1 : top + 1 + size_y])
        result = here - (flux_next - flux_ref[...]) - (g_next - g_here)
        flux_ref[...] = flux_next
        out_ref[pl.ds(pl.multiple_of(x * size_y, 8), size_y), :] = result

    def advect_inner(x, carry):
        advect(x, q_ref[x + 1], w_ref[x + 1][:, :levels])
        return carry

    lax.fori_loop(0, size_x - 1, advect_inner, 0)
    advect(size_x - 1, right_ref[:, :width], right_ref[:, width : width + levels])

    runs = pair_blocks(chan)
    per_chunk = DEPTH // ROWS
    nothing = jnp.zeros((ROWS, LANES), jnp.bfloat16)
    long = turned_ref.shape[0]

    def collide(block, carry):
        rows = pl.ds(pl.multiple_of(block * LANES, LANES), LANES)
        advected = out_ref[rows, :]
        turned_ref[...] = jnp.concatenate(
            [advected, jnp.zeros((LANES, long - width), jnp.float32)], axis=1
        ).T
        cloudy = mask_ref[block] > 0
        for level in range(0, levels, 2):
            starts = (level * chan, (level + 1) * chan)
            tiles = [
                [turned_ref[s + j : s + j + ROWS].astype(jnp.bfloat16) for j in range(0, chan, ROWS)]
                for s in starts
            ]
            total = jnp.zeros((fold_ref.shape[0], 2 * LANES), jnp.float32)
            for chunk in range(0, len(runs), per_chunk):
                halves = []
                for s, tile in zip(starts, tiles):
                    made = []
                    for i, j in runs[chunk : chunk + per_chunk]:
                        one = jnp.broadcast_to(turned_ref[s + i : s + i + 1], (ROWS, LANES)).astype(jnp.bfloat16)
                        made.append(one * tile[j // ROWS])
                    made += [nothing] * (per_chunk - len(made))
                    halves.append(jnp.concatenate(made, axis=0))
                pairs = jnp.concatenate(halves, axis=1)
                columns = slice(chunk * ROWS, chunk * ROWS + DEPTH)
                total += jnp.dot(fold_ref[:, columns], pairs, preferred_element_type=jnp.float32)
            rounded = total.astype(jnp.bfloat16).astype(jnp.float32)
            for half, s in enumerate(starts):
                kept = rounded[:chan, half * LANES : (half + 1) * LANES]
                back_ref[s : s + chan] = jnp.where(cloudy, kept, 0.0)
        out_ref[rows, :] = advected + back_ref[...].T[:, :width]
        return carry

    back_ref[...] = jnp.zeros_like(back_ref)
    lax.fori_loop(0, size_x * size_y // LANES, collide, 0)


def per_device(hydro, winds, cloud_mask, coal_kernel, block_mask):
    size_x, size_y, width = hydro.shape
    levels = winds.shape[2] // 2
    chan = width // levels
    sides = []
    for axis, dim in (("gx", 0), ("gy", 1)):
        shape = (size_y, -1) if dim == 0 else (size_x, 1, -1)
        last, first, up, down = edges(hydro, axis, dim)
        wlast, wfirst, _, _ = edges(winds, axis, dim)
        sides.append(lax.ppermute(jnp.concatenate([last, wlast], axis=1), axis, up).reshape(shape))
        sides.append(lax.ppermute(jnp.concatenate([first, wfirst], axis=1), axis, down).reshape(shape))
    fold = folded_kernel(coal_kernel, block_mask, chan)
    onto = (jnp.arange(levels)[:, None] == jnp.arange(width)[None, :] // chan).astype(jnp.bfloat16)
    onto = jnp.concatenate([onto] * 3, axis=0)
    mask = cloud_mask.reshape(-1, 1, LANES)
    long = round_up(width, LANES)
    result = pl.pallas_call(
        lambda *refs: step_kernel(levels, chan, *refs),
        out_shape=jax.ShapeDtypeStruct((size_x * size_y, width), jnp.float32),
        in_specs=[pl.BlockSpec(memory_space=pltpu.VMEM)] * 9,
        out_specs=pl.BlockSpec(memory_space=pltpu.VMEM),
        scratch_shapes=[
            pltpu.VMEM((long, LANES), jnp.float32),
            pltpu.VMEM((long, LANES), jnp.float32),
            pltpu.VMEM((size_y, width), jnp.float32),
            pltpu.VMEM((size_y + 16, width), jnp.float32),
            pltpu.VMEM((size_y + 16, 2 * levels), jnp.float32),
        ],
        compiler_params=pltpu.CompilerParams(vmem_limit_bytes=40 * 2**20),
    )(hydro, winds, *sides, mask, onto, fold)
    return result.reshape(size_x, size_y, width)


def solution(mesh):
    in_specs = (P("gx", "gy", None), P("gx", "gy", None), P("gx", "gy"), P(), P())
    out_specs = P("gx", "gy", None)
    return jax.shard_map(
        per_device, mesh=mesh, in_specs=in_specs, out_specs=out_specs, check_vma=False
    )
```

```python
import jax
import jax.numpy as jnp
from jax import lax
from jax.experimental import pallas as pl
from jax.experimental.pallas import tpu as pltpu
from jax.sharding import PartitionSpec as P

BLK = 11
ROWS = 16
LANES = 128
DEPTH = 256


def round_up(value, unit):
    return (value + unit - 1) // unit * unit


def edges(array, axis, dim):
    count, length = lax.axis_size(axis), array.shape[dim]
    up = [(i, (i + 1) % count) for i in range(count)]
    down = [(j, i) for i, j in up]
    last = lax.index_in_dim(array, length - 1, dim, keepdims=dim > 0)
    first = lax.index_in_dim(array, 0, dim, keepdims=dim > 0)
    return last, first, up, down


def fold_kernel(chan, blocks_ref, cube_ref, out_ref, natural_ref, rows_ref, ahead_ref, back_ref):
    whole = chan // ROWS * ROWS
    count = blocks_ref.shape[0]
    total = chan * chan
    for first in range(0, total, LANES):
        length = min(LANES, total - first)
        piece = cube_ref[:, first : first + length].astype(jnp.float32)
        if length < LANES:
            piece = jnp.concatenate([piece, jnp.zeros((chan, LANES - length), jnp.float32)], axis=1)
        piece = jnp.concatenate([piece, jnp.zeros((LANES - chan, LANES), jnp.float32)], axis=0)
        natural_ref[first : first + LANES] = piece.T
    block_of = lax.broadcasted_iota(jnp.int32, ahead_ref.shape[1:], 0) // BLK
    for one in range(count):
        ahead = jnp.zeros(block_of.shape, jnp.float32)
        back = ahead
        for other in range(count):
            ahead = jnp.where(block_of == other, (blocks_ref[one, other] > 0).astype(jnp.float32), ahead)
            back = jnp.where(block_of == other, (blocks_ref[other, one] > 0).astype(jnp.float32), back)
        ahead_ref[one] = ahead
        back_ref[one] = back

    def forward(i, start, stop):
        return natural_ref[i * chan + start : i * chan + stop] * ahead_ref[i // BLK, start:stop]

    def backward(i, start, stop):
        taken = natural_ref[pl.ds(start * chan + i, stop - start, stride=chan), :]
        return taken * back_ref[i // BLK, start:stop]

    at = 0
    for i in range(whole):
        start = i // ROWS * ROWS
        rows_ref[at : at + ROWS] = forward(i, start, start + ROWS)
        at += ROWS
        start += ROWS
        if start < whole:
            rows_ref[at : at + whole - start] = forward(i, start, whole) + backward(i, start, whole)
            at += whole - start
    for i in range(whole, chan):
        rows_ref[at : at + whole] = forward(i, 0, whole) + backward(i, 0, whole)
        at += whole
    for i in range(whole, chan):
        rows_ref[at : at + ROWS] = jnp.zeros((ROWS, LANES), jnp.float32)
        rows_ref[at : at + chan - whole] = forward(i, whole, chan)
        at += ROWS
    rows_ref[at:] = jnp.zeros((rows_ref.shape[0] - at, LANES), jnp.float32)
    for first in range(0, rows_ref.shape[0], LANES):
        turned = rows_ref[first : first + LANES].T
        out_ref[:, first : first + LANES] = turned[: out_ref.shape[0]].astype(jnp.bfloat16)


def folded_kernel(coal_kernel, block_mask, chan):
    depth = round_up(len(pair_blocks(chan)) * ROWS, DEPTH)
    blocks = block_mask.shape[0]
    return pl.pallas_call(
        lambda *refs: fold_kernel(chan, *refs),
        out_shape=jax.ShapeDtypeStruct((round_up(chan, ROWS), depth), jnp.bfloat16),
        in_specs=[pl.BlockSpec(memory_space=pltpu.SMEM), pl.BlockSpec(memory_space=pltpu.VMEM)],
        out_specs=pl.BlockSpec(memory_space=pltpu.VMEM),
        scratch_shapes=[
            pltpu.VMEM((round_up(chan * chan, LANES), LANES), jnp.float32),
            pltpu.VMEM((depth, LANES), jnp.float32),
            pltpu.VMEM((blocks, round_up(chan, 8), LANES), jnp.float32),
            pltpu.VMEM((blocks, round_up(chan, 8), LANES), jnp.float32),
        ],
        cost_estimate=pl.CostEstimate(flops=2**25, bytes_accessed=2**22, transcendentals=0),
        compiler_params=pltpu.CompilerParams(vmem_limit_bytes=16 * 2**20),
    )(block_mask, coal_kernel.T)


def pair_blocks(chan):
    whole = chan // ROWS * ROWS
    runs = [(i, j) for i in range(whole) for j in range(i // ROWS * ROWS, whole, ROWS)]
    runs += [(i, j) for i in range(whole, chan) for j in range(0, whole, ROWS)]
    runs += [(i, whole) for i in range(whole, chan)]
    return runs


def three_parts(value):
    high = value.astype(jnp.bfloat16)
    rest = value - high.astype(jnp.float32)
    middle = rest.astype(jnp.bfloat16)
    low = (rest - middle.astype(jnp.float32)).astype(jnp.bfloat16)
    return jnp.concatenate([high, middle, low], axis=1)


def step_kernel(levels, chan, q_ref, w_ref, left_ref, right_ref, below_ref, above_ref, mask_ref, spread_ref, fold_ref,
                out_ref, turned_ref, back_ref, flux_ref, tall_ref, wtall_ref):
    size_x, size_y, width = q_ref.shape
    top = 8

    def spread(face):
        return jnp.dot(three_parts(face), spread_ref[...], preferred_element_type=jnp.float32)

    def upwind(face, before, after):
        return jnp.maximum(face, 0.0) * before + jnp.minimum(face, 0.0) * after

    u_first = w_ref[0][:, :levels]
    face = spread(0.5 * (left_ref[:, width : width + levels] + u_first))
    flux_ref[...] = upwind(face, left_ref[:, :width], q_ref[0])

    def advect(x, q_next, u_next):
        here = q_ref[x]
        winds = w_ref[x]
        tall_ref[top : top + size_y] = here
        tall_ref[top - 1 : top] = below_ref[x][:, :width]
        tall_ref[top + size_y : top + size_y + 1] = above_ref[x][:, :width]
        wtall_ref[top : top + size_y] = winds
        wtall_ref[top - 1 : top] = below_ref[x][:, width:]
        wtall_ref[top + size_y : top + size_y + 1] = above_ref[x][:, width:]
        v = winds[:, levels:]
        v_before = wtall_ref[top - 1 : top - 1 + size_y][:, levels:]
        v_after = wtall_ref[top + 1 : top + 1 + size_y][:, levels:]
        faces = jnp.concatenate(
            [0.5 * (winds[:, :levels] + u_next), 0.5 * (v_before + v), 0.5 * (v + v_after)], axis=0
        )
        wide = spread(faces)
        flux_next = upwind(wide[:size_y], here, q_next)
        g_here = upwind(wide[size_y : 2 * size_y], tall_ref[top - 1 : top - 1 + size_y], here)
        g_next = upwind(wide[2 * size_y :], here, tall_ref[top + 1 : top + 1 + size_y])
        result = here - (flux_next - flux_ref[...]) - (g_next - g_here)
        flux_ref[...] = flux_next
        out_ref[pl.ds(pl.multiple_of(x * size_y, 8), size_y), :] = result

    def advect_inner(x, carry):
        advect(x, q_ref[x + 1], w_ref[x + 1][:, :levels])
        return carry

    lax.fori_loop(0, size_x - 1, advect_inner, 0)
    advect(size_x - 1, right_ref[:, :width], right_ref[:, width : width + levels])

    runs = pair_blocks(chan)
    per_chunk = DEPTH // ROWS
    nothing = jnp.zeros((ROWS, LANES), jnp.bfloat16)
    long = turned_ref.shape[0]

    def collide(block, carry):
        rows = pl.ds(pl.multiple_of(block * LANES, LANES), LANES)
        advected = out_ref[rows, :]
        turned_ref[...] = jnp.concatenate(
            [advected, jnp.zeros((LANES, long - width), jnp.float32)], axis=1
        ).T
        cloudy = mask_ref[block] > 0
        for level in range(0, levels, 2):
            starts = (level * chan, (level + 1) * chan)
            tiles = [
                [turned_ref[s + j : s + j + ROWS].astype(jnp.bfloat16) for j in range(0, chan, ROWS)]
                for s in starts
            ]
            total = jnp.zeros((fold_ref.shape[0], 2 * LANES), jnp.float32)
            for chunk in range(0, len(runs), per_chunk):
                halves = []
                for s, tile in zip(starts, tiles):
                    made = []
                    for i, j in runs[chunk : chunk + per_chunk]:
                        one = jnp.broadcast_to(turned_ref[s + i : s + i + 1], (ROWS, LANES)).astype(jnp.bfloat16)
                        made.append(one * tile[j // ROWS])
                    made += [nothing] * (per_chunk - len(made))
                    halves.append(jnp.concatenate(made, axis=0))
                pairs = jnp.concatenate(halves, axis=1)
                columns = slice(chunk * ROWS, chunk * ROWS + DEPTH)
                total += jnp.dot(fold_ref[:, columns], pairs, preferred_element_type=jnp.float32)
            rounded = total.astype(jnp.bfloat16).astype(jnp.float32)
            for half, s in enumerate(starts):
                kept = rounded[:chan, half * LANES : (half + 1) * LANES]
                back_ref[s : s + chan] = jnp.where(cloudy, kept, 0.0)
        out_ref[rows, :] = advected + back_ref[...].T[:, :width]
        return carry

    back_ref[...] = jnp.zeros_like(back_ref)
    lax.fori_loop(0, size_x * size_y // LANES, collide, 0)


def per_device(hydro, winds, cloud_mask, coal_kernel, block_mask):
    size_x, size_y, width = hydro.shape
    levels = winds.shape[2] // 2
    chan = width // levels
    sides = []
    for axis, dim in (("gx", 0), ("gy", 1)):
        last, first, up, down = edges(hydro, axis, dim)
        wlast, wfirst, _, _ = edges(winds, axis, dim)
        sides.append(lax.ppermute(jnp.concatenate([last, wlast], axis=-1), axis, up))
        sides.append(lax.ppermute(jnp.concatenate([first, wfirst], axis=-1), axis, down))
    fold = folded_kernel(coal_kernel, block_mask, chan)
    onto = (jnp.arange(levels)[:, None] == jnp.arange(width)[None, :] // chan).astype(jnp.bfloat16)
    onto = jnp.concatenate([onto] * 3, axis=0)
    mask = cloud_mask.reshape(-1, 1, LANES)
    long = round_up(width, LANES)
    result = pl.pallas_call(
        lambda *refs: step_kernel(levels, chan, *refs),
        out_shape=jax.ShapeDtypeStruct((size_x * size_y, width), jnp.float32),
        in_specs=[pl.BlockSpec(memory_space=pltpu.VMEM)] * 9,
        out_specs=pl.BlockSpec(memory_space=pltpu.VMEM),
        scratch_shapes=[
            pltpu.VMEM((long, LANES), jnp.float32),
            pltpu.VMEM((long, LANES), jnp.float32),
            pltpu.VMEM((size_y, width), jnp.float32),
            pltpu.VMEM((size_y + 16, width), jnp.float32),
            pltpu.VMEM((size_y + 16, 2 * levels), jnp.float32),
        ],
        compiler_params=pltpu.CompilerParams(vmem_limit_bytes=40 * 2**20),
    )(hydro, winds, *sides, mask, onto, fold)
    return result.reshape(size_x, size_y, width)


def solution(mesh):
    in_specs = (P("gx", "gy", None), P("gx", "gy", None), P("gx", "gy"), P(), P())
    out_specs = P("gx", "gy", None)
    return jax.shard_map(
        per_device, mesh=mesh, in_specs=in_specs, out_specs=out_specs, check_vma=False
    )
```

```python
import jax
import jax.numpy as jnp
from jax import lax
from jax.experimental import pallas as pl
from jax.experimental.pallas import tpu as pltpu
from jax.sharding import PartitionSpec as P

BLK = 11
ROWS = 16
LANES = 128
DEPTH = 256


def round_up(value, unit):
    return (value + unit - 1) // unit * unit


def halo_kernel(axes, q_ref, w_ref, left_ref, right_ref, below_ref, above_ref, x_rows, y_rows, x_out, y_out, x_in, y_in,
                near_sem, send_sem, recv_sem):
    size_x, size_y, width = q_ref.shape
    faces = w_ref.shape[2]
    wide = round_up(width, LANES)
    near = [
        pltpu.make_async_copy(q_ref.at[size_x - 1], x_rows.at[0], near_sem.at[0]),
        pltpu.make_async_copy(q_ref.at[0], x_rows.at[1], near_sem.at[1]),
        pltpu.make_async_copy(q_ref.at[:, size_y - 8 : size_y], y_rows.at[0], near_sem.at[2]),
        pltpu.make_async_copy(q_ref.at[:, 0:8], y_rows.at[1], near_sem.at[3]),
    ]
    for copy in near:
        copy.start()
    me = [lax.axis_index(axis) for axis, _ in axes]
    sides = []
    for spot, (_, count) in enumerate(axes):
        for move in (1, count - 1):
            place = list(me)
            place[spot] = lax.rem(me[spot] + move, count)
            sides.append(tuple(place))
    barrier = pltpu.get_barrier_semaphore()
    for side in sides:
        pl.semaphore_signal(barrier, inc=1, device_id=side, device_id_type=pl.DeviceIdType.MESH)
    x_out[...] = jnp.zeros_like(x_out)
    y_out[...] = jnp.zeros_like(y_out)
    for copy in near:
        copy.wait()
    for k, x in enumerate((size_x - 1, 0)):
        x_out[k, :, :width] = x_rows[k]
        x_out[k, :, wide : wide + faces] = w_ref[x]

    def pick(x, carry):
        for k, (row, y) in enumerate(((7, size_y - 1), (0, 0))):
            y_out[k, x, :, :width] = y_rows[k, x][row : row + 1]
            y_out[k, x, :, wide : wide + faces] = w_ref[x][y : y + 1]
        return carry

    lax.fori_loop(0, size_x, pick, 0)
    pl.semaphore_wait(barrier, len(sides))
    moves = []
    for k, side in enumerate(sides):
        out, into = (x_out, x_in) if k < 2 else (y_out, y_in)
        moves.append(
            pltpu.make_async_remote_copy(
                src_ref=out.at[k % 2],
                dst_ref=into.at[k % 2],
                send_sem=send_sem.at[k],
                recv_sem=recv_sem.at[k],
                device_id=side,
                device_id_type=pl.DeviceIdType.MESH,
            )
        )
    for move in moves:
        move.start()
    for move in moves:
        move.wait()
    left_ref[...] = x_in[0]
    right_ref[...] = x_in[1]
    below_ref[...] = y_in[0]
    above_ref[...] = y_in[1]


def halos(hydro, winds):
    size_x, size_y, width = hydro.shape
    long = round_up(width, LANES) + round_up(winds.shape[2], LANES)
    axes = tuple((axis, lax.axis_size(axis)) for axis in ("gx", "gy"))
    along_x, along_y = (size_y, long), (size_x, 1, long)
    return pl.pallas_call(
        lambda *refs: halo_kernel(axes, *refs),
        out_shape=[jax.ShapeDtypeStruct(shape, jnp.float32) for shape in (along_x, along_x, along_y, along_y)],
        in_specs=[pl.BlockSpec(memory_space=pl.ANY), pl.BlockSpec(memory_space=pltpu.VMEM)],
        out_specs=[pl.BlockSpec(memory_space=pltpu.VMEM)] * 4,
        scratch_shapes=[
            pltpu.VMEM((2, size_y, width), jnp.float32),
            pltpu.VMEM((2, size_x, 8, width), jnp.float32),
            pltpu.VMEM((2,) + along_x, jnp.float32),
            pltpu.VMEM((2,) + along_y, jnp.float32),
            pltpu.VMEM((2,) + along_x, jnp.float32),
            pltpu.VMEM((2,) + along_y, jnp.float32),
            pltpu.SemaphoreType.DMA((4,)),
            pltpu.SemaphoreType.DMA((4,)),
            pltpu.SemaphoreType.DMA((4,)),
        ],
        compiler_params=pltpu.CompilerParams(
            collective_id=0, has_side_effects=True, vmem_limit_bytes=56 * 2**20
        ),
    )(hydro, winds)


def fold_kernel(chan, blocks_ref, cube_ref, out_ref, natural_ref, rows_ref, ahead_ref, back_ref):
    whole = chan // ROWS * ROWS
    count = blocks_ref.shape[0]
    total = chan * chan
    for first in range(0, total, LANES):
        length = min(LANES, total - first)
        piece = cube_ref[:, first : first + length].astype(jnp.float32)
        if length < LANES:
            piece = jnp.concatenate([piece, jnp.zeros((chan, LANES - length), jnp.float32)], axis=1)
        piece = jnp.concatenate([piece, jnp.zeros((LANES - chan, LANES), jnp.float32)], axis=0)
        natural_ref[first : first + LANES] = piece.T
    block_of = lax.broadcasted_iota(jnp.int32, ahead_ref.shape[1:], 0) // BLK
    for one in range(count):
        ahead = jnp.zeros(block_of.shape, jnp.float32)
        back = ahead
        for other in range(count):
            ahead = jnp.where(block_of == other, (blocks_ref[one, other] > 0).astype(jnp.float32), ahead)
            back = jnp.where(block_of == other, (blocks_ref[other, one] > 0).astype(jnp.float32), back)
        ahead_ref[one] = ahead
        back_ref[one] = back

    def forward(i, start, stop):
        return natural_ref[i * chan + start : i * chan + stop] * ahead_ref[i // BLK, start:stop]

    def backward(i, start, stop):
        taken = natural_ref[pl.ds(start * chan + i, stop - start, stride=chan), :]
        return taken * back_ref[i // BLK, start:stop]

    at = 0
    for i in range(whole):
        start = i // ROWS * ROWS
        rows_ref[at : at + ROWS] = forward(i, start, start + ROWS)
        at += ROWS
        start += ROWS
        if start < whole:
            rows_ref[at : at + whole - start] = forward(i, start, whole) + backward(i, start, whole)
            at += whole - start
    for i in range(whole, chan):
        rows_ref[at : at + whole] = forward(i, 0, whole) + backward(i, 0, whole)
        at += whole
    for i in range(whole, chan):
        rows_ref[at : at + ROWS] = jnp.zeros((ROWS, LANES), jnp.float32)
        rows_ref[at : at + chan - whole] = forward(i, whole, chan)
        at += ROWS
    rows_ref[at:] = jnp.zeros((rows_ref.shape[0] - at, LANES), jnp.float32)
    for first in range(0, rows_ref.shape[0], LANES):
        turned = rows_ref[first : first + LANES].T
        out_ref[:, first : first + LANES] = turned[: out_ref.shape[0]].astype(jnp.bfloat16)


def folded_kernel(coal_kernel, block_mask, chan):
    depth = round_up(len(pair_blocks(chan)) * ROWS, DEPTH)
    blocks = block_mask.shape[0]
    return pl.pallas_call(
        lambda *refs: fold_kernel(chan, *refs),
        out_shape=jax.ShapeDtypeStruct((round_up(chan, ROWS), depth), jnp.bfloat16),
        in_specs=[pl.BlockSpec(memory_space=pltpu.SMEM), pl.BlockSpec(memory_space=pltpu.VMEM)],
        out_specs=pl.BlockSpec(memory_space=pltpu.VMEM),
        scratch_shapes=[
            pltpu.VMEM((round_up(chan * chan, LANES), LANES), jnp.float32),
            pltpu.VMEM((depth, LANES), jnp.float32),
            pltpu.VMEM((blocks, round_up(chan, 8), LANES), jnp.float32),
            pltpu.VMEM((blocks, round_up(chan, 8), LANES), jnp.float32),
        ],
        cost_estimate=pl.CostEstimate(flops=2**25, bytes_accessed=2**22, transcendentals=0),
        compiler_params=pltpu.CompilerParams(vmem_limit_bytes=16 * 2**20),
    )(block_mask, coal_kernel.T)


def pair_blocks(chan):
    whole = chan // ROWS * ROWS
    runs = [(i, j) for i in range(whole) for j in range(i // ROWS * ROWS, whole, ROWS)]
    runs += [(i, j) for i in range(whole, chan) for j in range(0, whole, ROWS)]
    runs += [(i, whole) for i in range(whole, chan)]
    return runs


def three_parts(value):
    high = value.astype(jnp.bfloat16)
    rest = value - high.astype(jnp.float32)
    middle = rest.astype(jnp.bfloat16)
    low = (rest - middle.astype(jnp.float32)).astype(jnp.bfloat16)
    return jnp.concatenate([high, middle, low], axis=1)


def step_kernel(levels, chan, q_hbm, w_ref, left_ref, right_ref, below_ref, above_ref, mask_ref, spread_ref, fold_ref,
                out_hbm, turned_ref, back_ref, flux_ref, tall_ref, wtall_ref, q_ref, out_ref, in_sem, out_sem):
    size_x, size_y, width = q_ref.shape

    def fetch(x):
        return pltpu.make_async_copy(q_hbm.at[x], q_ref.at[x], in_sem.at[x])

    def keep(block):
        rows = pl.ds(pl.multiple_of(block * LANES, LANES), LANES)
        return pltpu.make_async_copy(out_ref.at[rows], out_hbm.at[rows], out_sem.at[block])

    def start_fetch(x, carry):
        fetch(x).start()
        return carry

    lax.fori_loop(0, size_x, start_fetch, 0)
    fetch(0).wait()
    top = 8
    wide_at = round_up(width, LANES)

    def spread(face):
        return jnp.dot(three_parts(face), spread_ref[...], preferred_element_type=jnp.float32)

    def upwind(face, before, after):
        return jnp.maximum(face, 0.0) * before + jnp.minimum(face, 0.0) * after

    u_first = w_ref[0][:, :levels]
    face = spread(0.5 * (left_ref[:, wide_at : wide_at + levels] + u_first))
    flux_ref[...] = upwind(face, left_ref[:, :width], q_ref[0])

    def advect(x, q_next, u_next):
        here = q_ref[x]
        winds = w_ref[x]
        tall_ref[top : top + size_y] = here
        tall_ref[top - 1 : top] = below_ref[x][:, :width]
        tall_ref[top + size_y : top + size_y + 1] = above_ref[x][:, :width]
        wtall_ref[top : top + size_y] = winds
        wtall_ref[top - 1 : top] = below_ref[x][:, wide_at : wide_at + 2 * levels]
        wtall_ref[top + size_y : top + size_y + 1] = above_ref[x][:, wide_at : wide_at + 2 * levels]
        v = winds[:, levels:]
        v_before = wtall_ref[top - 1 : top - 1 + size_y][:, levels:]
        v_after = wtall_ref[top + 1 : top + 1 + size_y][:, levels:]
        faces = jnp.concatenate(
            [0.5 * (winds[:, :levels] + u_next), 0.5 * (v_before + v), 0.5 * (v + v_after)], axis=0
        )
        wide = spread(faces)
        flux_next = upwind(wide[:size_y], here, q_next)
        g_here = upwind(wide[size_y : 2 * size_y], tall_ref[top - 1 : top - 1 + size_y], here)
        g_next = upwind(wide[2 * size_y :], here, tall_ref[top + 1 : top + 1 + size_y])
        result = here - (flux_next - flux_ref[...]) - (g_next - g_here)
        flux_ref[...] = flux_next
        out_ref[pl.ds(pl.multiple_of(x * size_y, 8), size_y), :] = result

    def advect_inner(x, carry):
        fetch(x + 1).wait()
        advect(x, q_ref[x + 1], w_ref[x + 1][:, :levels])
        return carry

    lax.fori_loop(0, size_x - 1, advect_inner, 0)
    advect(size_x - 1, right_ref[:, :width], right_ref[:, wide_at : wide_at + levels])

    runs = pair_blocks(chan)
    per_chunk = DEPTH // ROWS
    nothing = jnp.zeros((ROWS, LANES), jnp.bfloat16)
    long = turned_ref.shape[0]

    def collide(block, carry):
        rows = pl.ds(pl.multiple_of(block * LANES, LANES), LANES)
        advected = out_ref[rows, :]
        turned_ref[...] = jnp.concatenate(
            [advected, jnp.zeros((LANES, long - width), jnp.float32)], axis=1
        ).T
        cloudy = mask_ref[block] > 0
        for level in range(0, levels, 2):
            starts = (level * chan, (level + 1) * chan)
            tiles = [
                [turned_ref[s + j : s + j + ROWS].astype(jnp.bfloat16) for j in range(0, chan, ROWS)]
                for s in starts
            ]
            total = jnp.zeros((fold_ref.shape[0], 2 * LANES), jnp.float32)
            for chunk in range(0, len(runs), per_chunk):
                halves = []
                for s, tile in zip(starts, tiles):
                    made = []
                    for i, j in runs[chunk : chunk + per_chunk]:
                        one = jnp.broadcast_to(turned_ref[s + i : s + i + 1], (ROWS, LANES)).astype(jnp.bfloat16)
                        made.append(one * tile[j // ROWS])
                    made += [nothing] * (per_chunk - len(made))
                    halves.append(jnp.concatenate(made, axis=0))
                pairs = jnp.concatenate(halves, axis=1)
                columns = slice(chunk * ROWS, chunk * ROWS + DEPTH)
                total += jnp.dot(fold_ref[:, columns], pairs, preferred_element_type=jnp.float32)
            rounded = total.astype(jnp.bfloat16).astype(jnp.float32)
            for half, s in enumerate(starts):
                kept = rounded[:chan, half * LANES : (half + 1) * LANES]
                back_ref[s : s + chan] = jnp.where(cloudy, kept, 0.0)
        out_ref[rows, :] = advected + back_ref[...].T[:, :width]
        keep(block).start()
        return carry

    back_ref[...] = jnp.zeros_like(back_ref)
    blocks = size_x * size_y // LANES
    lax.fori_loop(0, blocks, collide, 0)

    def finish(block, carry):
        keep(block).wait()
        return carry

    lax.fori_loop(0, blocks, finish, 0)


def per_device(hydro, winds, cloud_mask, coal_kernel, block_mask):
    size_x, size_y, width = hydro.shape
    levels = winds.shape[2] // 2
    chan = width // levels
    sides = halos(hydro, winds)
    fold = folded_kernel(coal_kernel, block_mask, chan)
    onto = (jnp.arange(levels)[:, None] == jnp.arange(width)[None, :] // chan).astype(jnp.bfloat16)
    onto = jnp.concatenate([onto] * 3, axis=0)
    mask = cloud_mask.reshape(-1, 1, LANES)
    long = round_up(width, LANES)
    result = pl.pallas_call(
        lambda *refs: step_kernel(levels, chan, *refs),
        out_shape=jax.ShapeDtypeStruct((size_x * size_y, width), jnp.float32),
        in_specs=[pl.BlockSpec(memory_space=pl.ANY)] + [pl.BlockSpec(memory_space=pltpu.VMEM)] * 8,
        out_specs=pl.BlockSpec(memory_space=pl.ANY),
        scratch_shapes=[
            pltpu.VMEM((long, LANES), jnp.float32),
            pltpu.VMEM((long, LANES), jnp.float32),
            pltpu.VMEM((size_y, width), jnp.float32),
            pltpu.VMEM((size_y + 16, width), jnp.float32),
            pltpu.VMEM((size_y + 16, 2 * levels), jnp.float32),
            pltpu.VMEM((size_x, size_y, width), jnp.float32),
            pltpu.VMEM((size_x * size_y, width), jnp.float32),
            pltpu.SemaphoreType.DMA((size_x,)),
            pltpu.SemaphoreType.DMA((size_x * size_y // LANES,)),
        ],
        compiler_params=pltpu.CompilerParams(vmem_limit_bytes=56 * 2**20),
    )(hydro, winds, *sides, mask, onto, fold)
    return result.reshape(size_x, size_y, width)


def solution(mesh):
    in_specs = (P("gx", "gy", None), P("gx", "gy", None), P("gx", "gy"), P(), P())
    out_specs = P("gx", "gy", None)
    return jax.shard_map(
        per_device, mesh=mesh, in_specs=in_specs, out_specs=out_specs, check_vma=False
    )
```

```python
import jax
import jax.numpy as jnp
from jax import lax
from jax.experimental import pallas as pl
from jax.experimental.pallas import tpu as pltpu
from jax.sharding import PartitionSpec as P

BLK = 11
ROWS = 16
LANES = 128
DEPTH = 256


def round_up(value, unit):
    return (value + unit - 1) // unit * unit


def edges(array, axis, dim):
    count, length = lax.axis_size(axis), array.shape[dim]
    up = [(i, (i + 1) % count) for i in range(count)]
    down = [(j, i) for i, j in up]
    last = lax.index_in_dim(array, length - 1, dim, keepdims=dim > 0)
    first = lax.index_in_dim(array, 0, dim, keepdims=dim > 0)
    return last, first, up, down


def fold_kernel(chan, blocks_ref, cube_ref, out_ref, natural_ref, rows_ref, ahead_ref, back_ref):
    whole = chan // ROWS * ROWS
    count = blocks_ref.shape[0]
    total = chan * chan
    for first in range(0, total, LANES):
        length = min(LANES, total - first)
        piece = cube_ref[:, first : first + length].astype(jnp.float32)
        if length < LANES:
            piece = jnp.concatenate([piece, jnp.zeros((chan, LANES - length), jnp.float32)], axis=1)
        piece = jnp.concatenate([piece, jnp.zeros((LANES - chan, LANES), jnp.float32)], axis=0)
        natural_ref[first : first + LANES] = piece.T
    block_of = lax.broadcasted_iota(jnp.int32, ahead_ref.shape[1:], 0) // BLK
    for one in range(count):
        ahead = jnp.zeros(block_of.shape, jnp.float32)
        back = ahead
        for other in range(count):
            ahead = jnp.where(block_of == other, (blocks_ref[one, other] > 0).astype(jnp.float32), ahead)
            back = jnp.where(block_of == other, (blocks_ref[other, one] > 0).astype(jnp.float32), back)
        ahead_ref[one] = ahead
        back_ref[one] = back

    def forward(i, start, stop):
        return natural_ref[i * chan + start : i * chan + stop] * ahead_ref[i // BLK, start:stop]

    def backward(i, start, stop):
        taken = natural_ref[pl.ds(start * chan + i, stop - start, stride=chan), :]
        return taken * back_ref[i // BLK, start:stop]

    row = lax.broadcasted_iota(jnp.int32, (ROWS, LANES), 0)
    half = ROWS // 2
    at = 0
    for i in range(whole):
        start = i // ROWS * ROWS + ROWS
        if start < whole:
            rows_ref[at : at + whole - start] = forward(i, start, whole) + backward(i, start, whole)
            at += whole - start
    for start in range(0, whole, ROWS):
        for s in range(half):
            near = (row >= s) & (row < s + half)
            i, stop = start + s, start + ROWS
            there = jnp.where(near, forward(i, start, stop), forward(i + half, start, stop))
            back = jnp.where(near, backward(i, start, stop), backward(i + half, start, stop))
            same = (row == s) | (row == s + half)
            rows_ref[at : at + ROWS] = there + jnp.where(same, 0.0, back)
            at += ROWS
    for start in range(0, whole, ROWS):
        for i in range(start, start + half):
            j = i + half
            rows_ref[at : at + 1] = forward(i, j, j + 1) + forward(j, i, i + 1)
            at += 1
    for i in range(whole, chan):
        rows_ref[at : at + whole] = forward(i, 0, whole) + backward(i, 0, whole)
        at += whole
    for i in range(whole, chan):
        rows_ref[at : at + ROWS] = jnp.zeros((ROWS, LANES), jnp.float32)
        rows_ref[at : at + chan - whole] = forward(i, whole, chan)
        at += ROWS
    rows_ref[at:] = jnp.zeros((rows_ref.shape[0] - at, LANES), jnp.float32)
    for first in range(0, rows_ref.shape[0], LANES):
        turned = rows_ref[first : first + LANES].T
        out_ref[:, first : first + LANES] = turned[: out_ref.shape[0]].astype(jnp.bfloat16)


def folded_kernel(coal_kernel, block_mask, chan):
    depth = round_up(len(pair_blocks(chan)) * ROWS, DEPTH)
    blocks = block_mask.shape[0]
    return pl.pallas_call(
        lambda *refs: fold_kernel(chan, *refs),
        out_shape=jax.ShapeDtypeStruct((round_up(chan, ROWS), depth), jnp.bfloat16),
        in_specs=[pl.BlockSpec(memory_space=pltpu.SMEM), pl.BlockSpec(memory_space=pltpu.VMEM)],
        out_specs=pl.BlockSpec(memory_space=pltpu.VMEM),
        scratch_shapes=[
            pltpu.VMEM((round_up(chan * chan, LANES), LANES), jnp.float32),
            pltpu.VMEM((depth, LANES), jnp.float32),
            pltpu.VMEM((blocks, round_up(chan, 8), LANES), jnp.float32),
            pltpu.VMEM((blocks, round_up(chan, 8), LANES), jnp.float32),
        ],
        cost_estimate=pl.CostEstimate(flops=2**25, bytes_accessed=2**22, transcendentals=0),
        compiler_params=pltpu.CompilerParams(vmem_limit_bytes=16 * 2**20),
    )(block_mask, coal_kernel.T)


def pair_blocks(chan):
    whole = chan // ROWS * ROWS
    runs = [(0, i, j) for i in range(whole) for j in range(i // ROWS * ROWS + ROWS, whole, ROWS)]
    runs += [(1, start + s, start) for start in range(0, whole, ROWS) for s in range(ROWS // 2)]
    runs += [(2, start, start + ROWS) for start in range(0, whole, 2 * ROWS)]
    runs += [(0, i, j) for i in range(whole, chan) for j in range(0, whole, ROWS)]
    runs += [(0, i, whole) for i in range(whole, chan)]
    return runs


def three_parts(value):
    high = value.astype(jnp.bfloat16)
    rest = value - high.astype(jnp.float32)
    middle = rest.astype(jnp.bfloat16)
    low = (rest - middle.astype(jnp.float32)).astype(jnp.bfloat16)
    return jnp.concatenate([high, middle, low], axis=1)


def step_kernel(levels, chan, q_hbm, w_ref, left_ref, right_ref, below_ref, above_ref, mask_ref, spread_ref, fold_ref,
                out_hbm, turned_ref, back_ref, flux_ref, tall_ref, wtall_ref, q_ref, out_ref, in_sem, out_sem):
    size_x, size_y, width = q_ref.shape

    def fetch(x):
        return pltpu.make_async_copy(q_hbm.at[x], q_ref.at[x], in_sem.at[x])

    def keep(block):
        rows = pl.ds(pl.multiple_of(block * LANES, LANES), LANES)
        return pltpu.make_async_copy(out_ref.at[rows], out_hbm.at[rows], out_sem.at[block])

    def start_fetch(x, carry):
        fetch(x).start()
        return carry

    lax.fori_loop(0, size_x, start_fetch, 0)
    fetch(0).wait()
    top = 8

    def spread(face):
        return jnp.dot(three_parts(face), spread_ref[...], preferred_element_type=jnp.float32)

    def upwind(face, before, after):
        return jnp.maximum(face, 0.0) * before + jnp.minimum(face, 0.0) * after

    u_first = w_ref[0][:, :levels]
    face = spread(0.5 * (left_ref[:, width : width + levels] + u_first))
    flux_ref[...] = upwind(face, left_ref[:, :width], q_ref[0])

    def advect(x, q_next, u_next):
        here = q_ref[x]
        winds = w_ref[x]
        tall_ref[top : top + size_y] = here
        tall_ref[top - 1 : top] = below_ref[x][:, :width]
        tall_ref[top + size_y : top + size_y + 1] = above_ref[x][:, :width]
        wtall_ref[top : top + size_y] = winds
        wtall_ref[top - 1 : top] = below_ref[x][:, width:]
        wtall_ref[top + size_y : top + size_y + 1] = above_ref[x][:, width:]
        v = winds[:, levels:]
        v_before = wtall_ref[top - 1 : top - 1 + size_y][:, levels:]
        v_after = wtall_ref[top + 1 : top + 1 + size_y][:, levels:]
        faces = jnp.concatenate(
            [0.5 * (winds[:, :levels] + u_next), 0.5 * (v_before + v), 0.5 * (v + v_after)], axis=0
        )
        wide = spread(faces)
        flux_next = upwind(wide[:size_y], here, q_next)
        g_here = upwind(wide[size_y : 2 * size_y], tall_ref[top - 1 : top - 1 + size_y], here)
        g_next = upwind(wide[2 * size_y :], here, tall_ref[top + 1 : top + 1 + size_y])
        result = here - (flux_next - flux_ref[...]) - (g_next - g_here)
        flux_ref[...] = flux_next
        out_ref[pl.ds(pl.multiple_of(x * size_y, 8), size_y), :] = result

    def advect_inner(x, carry):
        fetch(x + 1).wait()
        advect(x, q_ref[x + 1], w_ref[x + 1][:, :levels])
        return carry

    lax.fori_loop(0, size_x - 1, advect_inner, 0)
    advect(size_x - 1, right_ref[:, :width], right_ref[:, width : width + levels])

    runs = pair_blocks(chan)
    per_chunk = DEPTH // ROWS
    nothing = jnp.zeros((ROWS, LANES), jnp.bfloat16)
    long = turned_ref.shape[0]
    row = lax.broadcasted_iota(jnp.int32, (ROWS, LANES), 0)

    def collide(block, carry):
        rows = pl.ds(pl.multiple_of(block * LANES, LANES), LANES)
        advected = out_ref[rows, :]
        turned_ref[...] = jnp.concatenate(
            [advected, jnp.zeros((LANES, long - width), jnp.float32)], axis=1
        ).T
        cloudy = mask_ref[block] > 0
        for level in range(0, levels, 2):
            starts = (level * chan, (level + 1) * chan)
            tiles = [
                [turned_ref[s + j : s + j + ROWS].astype(jnp.bfloat16) for j in range(0, chan, ROWS)]
                for s in starts
            ]
            total = jnp.zeros((fold_ref.shape[0], 2 * LANES), jnp.float32)
            for chunk in range(0, len(runs), per_chunk):
                halves = []
                for s, tile in zip(starts, tiles):
                    made = []
                    for kind, i, j in runs[chunk : chunk + per_chunk]:
                        if kind == 2:
                            parts = [tile[k // ROWS].astype(jnp.float32) for k in (i, j)]
                            parts = [part[: ROWS // 2] * part[ROWS // 2 :] for part in parts]
                            made.append(jnp.concatenate(parts, axis=0).astype(jnp.bfloat16))
                            continue
                        one = jnp.broadcast_to(turned_ref[s + i : s + i + 1], (ROWS, LANES))
                        if kind == 1:
                            k = i + ROWS // 2
                            far = jnp.broadcast_to(turned_ref[s + k : s + k + 1], (ROWS, LANES))
                            near = (row >= i - j) & (row < i - j + ROWS // 2)
                            one = jnp.where(near, one, far)
                        made.append(one.astype(jnp.bfloat16) * tile[j // ROWS])
                    made += [nothing] * (per_chunk - len(made))
                    halves.append(jnp.concatenate(made, axis=0))
                pairs = jnp.concatenate(halves, axis=1)
                columns = slice(chunk * ROWS, chunk * ROWS + DEPTH)
                total += jnp.dot(fold_ref[:, columns], pairs, preferred_element_type=jnp.float32)
            rounded = total.astype(jnp.bfloat16).astype(jnp.float32)
            for half, s in enumerate(starts):
                kept = rounded[:chan, half * LANES : (half + 1) * LANES]
                back_ref[s : s + chan] = jnp.where(cloudy, kept, 0.0)
        out_ref[rows, :] = advected + back_ref[...].T[:, :width]
        keep(block).start()
        return carry

    back_ref[...] = jnp.zeros_like(back_ref)
    blocks = size_x * size_y // LANES
    lax.fori_loop(0, blocks, collide, 0)

    def finish(block, carry):
        keep(block).wait()
        return carry

    lax.fori_loop(0, blocks, finish, 0)


def per_device(hydro, winds, cloud_mask, coal_kernel, block_mask):
    size_x, size_y, width = hydro.shape
    levels = winds.shape[2] // 2
    chan = width // levels
    sides = []
    for axis, dim in (("gx", 0), ("gy", 1)):
        last, first, up, down = edges(hydro, axis, dim)
        wlast, wfirst, _, _ = edges(winds, axis, dim)
        sides.append(lax.ppermute(jnp.concatenate([last, wlast], axis=-1), axis, up))
        sides.append(lax.ppermute(jnp.concatenate([first, wfirst], axis=-1), axis, down))
    fold = folded_kernel(coal_kernel, block_mask, chan)
    onto = (jnp.arange(levels)[:, None] == jnp.arange(width)[None, :] // chan).astype(jnp.bfloat16)
    onto = jnp.concatenate([onto] * 3, axis=0)
    mask = cloud_mask.reshape(-1, 1, LANES)
    long = round_up(width, LANES)
    result = pl.pallas_call(
        lambda *refs: step_kernel(levels, chan, *refs),
        out_shape=jax.ShapeDtypeStruct((size_x * size_y, width), jnp.float32),
        in_specs=[pl.BlockSpec(memory_space=pl.ANY)] + [pl.BlockSpec(memory_space=pltpu.VMEM)] * 8,
        out_specs=pl.BlockSpec(memory_space=pl.ANY),
        scratch_shapes=[
            pltpu.VMEM((long, LANES), jnp.float32),
            pltpu.VMEM((long, LANES), jnp.float32),
            pltpu.VMEM((size_y, width), jnp.float32),
            pltpu.VMEM((size_y + 16, width), jnp.float32),
            pltpu.VMEM((size_y + 16, 2 * levels), jnp.float32),
            pltpu.VMEM((size_x, size_y, width), jnp.float32),
            pltpu.VMEM((size_x * size_y, width), jnp.float32),
            pltpu.SemaphoreType.DMA((size_x,)),
            pltpu.SemaphoreType.DMA((size_x * size_y // LANES,)),
        ],
        compiler_params=pltpu.CompilerParams(vmem_limit_bytes=56 * 2**20),
    )(hydro, winds, *sides, mask, onto, fold)
    return result.reshape(size_x, size_y, width)


def solution(mesh):
    in_specs = (P("gx", "gy", None), P("gx", "gy", None), P("gx", "gy"), P(), P())
    out_specs = P("gx", "gy", None)
    return jax.shard_map(
        per_device, mesh=mesh, in_specs=in_specs, out_specs=out_specs, check_vma=False
    )
```

```python
import jax
import jax.numpy as jnp
from jax import lax
from jax.experimental import pallas as pl
from jax.experimental.pallas import tpu as pltpu
from jax.sharding import PartitionSpec as P

BLK = 11
ROWS = 16
LANES = 128
DEPTH = 256


def round_up(value, unit):
    return (value + unit - 1) // unit * unit


def edges(array, axis, dim):
    count, length = lax.axis_size(axis), array.shape[dim]
    up = [(i, (i + 1) % count) for i in range(count)]
    down = [(j, i) for i, j in up]
    last = lax.index_in_dim(array, length - 1, dim, keepdims=dim > 0)
    first = lax.index_in_dim(array, 0, dim, keepdims=dim > 0)
    return last, first, up, down


def fold_kernel(chan, blocks_ref, cube_ref, out_ref, natural_ref, rows_ref, ahead_ref, back_ref):
    whole = chan // ROWS * ROWS
    count = blocks_ref.shape[0]
    total = chan * chan
    for first in range(0, total, LANES):
        length = min(LANES, total - first)
        piece = cube_ref[:, first : first + length].astype(jnp.float32)
        if length < LANES:
            piece = jnp.concatenate([piece, jnp.zeros((chan, LANES - length), jnp.float32)], axis=1)
        piece = jnp.concatenate([piece, jnp.zeros((LANES - chan, LANES), jnp.float32)], axis=0)
        natural_ref[first : first + LANES] = piece.T
    block_of = lax.broadcasted_iota(jnp.int32, ahead_ref.shape[1:], 0) // BLK
    for one in range(count):
        ahead = jnp.zeros(block_of.shape, jnp.float32)
        back = ahead
        for other in range(count):
            ahead = jnp.where(block_of == other, (blocks_ref[one, other] > 0).astype(jnp.float32), ahead)
            back = jnp.where(block_of == other, (blocks_ref[other, one] > 0).astype(jnp.float32), back)
        ahead_ref[one] = ahead
        back_ref[one] = back

    def forward(i, start, stop):
        return natural_ref[i * chan + start : i * chan + stop] * ahead_ref[i // BLK, start:stop]

    def backward(i, start, stop):
        taken = natural_ref[pl.ds(start * chan + i, stop - start, stride=chan), :]
        return taken * back_ref[i // BLK, start:stop]

    row = lax.broadcasted_iota(jnp.int32, (ROWS, LANES), 0)
    half = ROWS // 2
    at = 0
    for i in range(whole):
        start = i // ROWS * ROWS + ROWS
        if start < whole:
            rows_ref[at : at + whole - start] = forward(i, start, whole) + backward(i, start, whole)
            at += whole - start
    for start in range(0, whole, ROWS):
        for s in range(half):
            near = (row >= s) & (row < s + half)
            i, stop = start + s, start + ROWS
            there = jnp.where(near, forward(i, start, stop), forward(i + half, start, stop))
            back = jnp.where(near, backward(i, start, stop), backward(i + half, start, stop))
            same = (row == s) | (row == s + half)
            rows_ref[at : at + ROWS] = there + jnp.where(same, 0.0, back)
            at += ROWS
    for start in range(0, whole, ROWS):
        for i in range(start, start + half):
            j = i + half
            rows_ref[at : at + 1] = forward(i, j, j + 1) + forward(j, i, i + 1)
            at += 1
    for i in range(whole, chan):
        rows_ref[at : at + whole] = forward(i, 0, whole) + backward(i, 0, whole)
        at += whole
    for i in range(whole, chan):
        rows_ref[at : at + ROWS] = jnp.zeros((ROWS, LANES), jnp.float32)
        rows_ref[at : at + chan - whole] = forward(i, whole, chan)
        at += ROWS
    rows_ref[at:] = jnp.zeros((rows_ref.shape[0] - at, LANES), jnp.float32)
    for first in range(0, rows_ref.shape[0], LANES):
        turned = rows_ref[first : first + LANES].T
        out_ref[:, first : first + LANES] = turned[: out_ref.shape[0]].astype(jnp.bfloat16)


def folded_kernel(coal_kernel, block_mask, chan):
    depth = round_up(len(pair_blocks(chan)) * ROWS, DEPTH)
    blocks = block_mask.shape[0]
    return pl.pallas_call(
        lambda *refs: fold_kernel(chan, *refs),
        out_shape=jax.ShapeDtypeStruct((round_up(chan, ROWS), depth), jnp.bfloat16),
        in_specs=[pl.BlockSpec(memory_space=pltpu.SMEM), pl.BlockSpec(memory_space=pltpu.VMEM)],
        out_specs=pl.BlockSpec(memory_space=pltpu.VMEM),
        scratch_shapes=[
            pltpu.VMEM((round_up(chan * chan, LANES), LANES), jnp.float32),
            pltpu.VMEM((depth, LANES), jnp.float32),
            pltpu.VMEM((blocks, round_up(chan, 8), LANES), jnp.float32),
            pltpu.VMEM((blocks, round_up(chan, 8), LANES), jnp.float32),
        ],
        cost_estimate=pl.CostEstimate(flops=2**25, bytes_accessed=2**22, transcendentals=0),
        compiler_params=pltpu.CompilerParams(vmem_limit_bytes=16 * 2**20),
    )(block_mask, coal_kernel.T)


def pair_blocks(chan):
    whole = chan // ROWS * ROWS
    runs = [(0, i, j) for i in range(whole) for j in range(i // ROWS * ROWS + ROWS, whole, ROWS)]
    runs += [(1, start + s, start) for start in range(0, whole, ROWS) for s in range(ROWS // 2)]
    runs += [(2, start, start + ROWS) for start in range(0, whole, 2 * ROWS)]
    runs += [(0, i, j) for i in range(whole, chan) for j in range(0, whole, ROWS)]
    runs += [(0, i, whole) for i in range(whole, chan)]
    return runs


def three_parts(value):
    high = value.astype(jnp.bfloat16)
    rest = value - high.astype(jnp.float32)
    middle = rest.astype(jnp.bfloat16)
    low = (rest - middle.astype(jnp.float32)).astype(jnp.bfloat16)
    return jnp.concatenate([high, middle, low], axis=1)


def step_kernel(levels, chan, q_hbm, w_ref, left_ref, right_ref, below_ref, above_ref, mask_ref, spread_ref, fold_ref,
                out_hbm, turned_ref, back_ref, flux_ref, tall_ref, wtall_ref, q_ref, out_ref, in_sem, out_sem):
    size_x, size_y, width = q_ref.shape

    def fetch(x):
        return pltpu.make_async_copy(q_hbm.at[x], q_ref.at[x], in_sem.at[x])

    def keep(block):
        rows = pl.ds(pl.multiple_of(block * LANES, LANES), LANES)
        return pltpu.make_async_copy(out_ref.at[rows], out_hbm.at[rows], out_sem.at[block])

    def start_fetch(x, carry):
        fetch(x).start()
        return carry

    lax.fori_loop(0, size_x, start_fetch, 0)
    fetch(0).wait()
    top = 8

    def spread(face):
        return jnp.dot(three_parts(face), spread_ref[...], preferred_element_type=jnp.float32)

    def upwind(face, before, after):
        return jnp.maximum(face, 0.0) * before + jnp.minimum(face, 0.0) * after

    left = left_ref[...].astype(jnp.float32)
    u_first = w_ref[0][:, :levels]
    face = spread(0.5 * (left[:, width : width + levels] + u_first))
    flux_ref[...] = upwind(face, left[:, :width], q_ref[0])

    def advect(x, q_next, u_next):
        here = q_ref[x]
        winds = w_ref[x]
        tall_ref[top : top + size_y] = here
        tall_ref[top - 1 : top] = below_ref[x][:, :width]
        tall_ref[top + size_y : top + size_y + 1] = above_ref[x][:, :width]
        wtall_ref[top : top + size_y] = winds
        wtall_ref[top - 1 : top] = below_ref[x][:, width:]
        wtall_ref[top + size_y : top + size_y + 1] = above_ref[x][:, width:]
        v = winds[:, levels:]
        v_before = wtall_ref[top - 1 : top - 1 + size_y][:, levels:]
        v_after = wtall_ref[top + 1 : top + 1 + size_y][:, levels:]
        faces = jnp.concatenate(
            [0.5 * (winds[:, :levels] + u_next), 0.5 * (v_before + v), 0.5 * (v + v_after)], axis=0
        )
        wide = spread(faces)
        flux_next = upwind(wide[:size_y], here, q_next)
        g_here = upwind(wide[size_y : 2 * size_y], tall_ref[top - 1 : top - 1 + size_y], here)
        g_next = upwind(wide[2 * size_y :], here, tall_ref[top + 1 : top + 1 + size_y])
        result = here - (flux_next - flux_ref[...]) - (g_next - g_here)
        flux_ref[...] = flux_next
        out_ref[pl.ds(pl.multiple_of(x * size_y, 8), size_y), :] = result

    def advect_inner(x, carry):
        fetch(x + 1).wait()
        advect(x, q_ref[x + 1], w_ref[x + 1][:, :levels])
        return carry

    lax.fori_loop(0, size_x - 1, advect_inner, 0)
    right = right_ref[...].astype(jnp.float32)
    advect(size_x - 1, right[:, :width], right[:, width : width + levels])

    runs = pair_blocks(chan)
    per_chunk = DEPTH // ROWS
    nothing = jnp.zeros((ROWS, LANES), jnp.bfloat16)
    long = turned_ref.shape[0]
    row = lax.broadcasted_iota(jnp.int32, (ROWS, LANES), 0)

    def collide(block, carry):
        rows = pl.ds(pl.multiple_of(block * LANES, LANES), LANES)
        advected = out_ref[rows, :]
        turned_ref[...] = jnp.concatenate(
            [advected, jnp.zeros((LANES, long - width), jnp.float32)], axis=1
        ).T
        cloudy = mask_ref[block] > 0
        for level in range(0, levels, 2):
            starts = (level * chan, (level + 1) * chan)
            tiles = [
                [turned_ref[s + j : s + j + ROWS].astype(jnp.bfloat16) for j in range(0, chan, ROWS)]
                for s in starts
            ]
            total = jnp.zeros((fold_ref.shape[0], 2 * LANES), jnp.float32)
            for chunk in range(0, len(runs), per_chunk):
                halves = []
                for s, tile in zip(starts, tiles):
                    made = []
                    for kind, i, j in runs[chunk : chunk + per_chunk]:
                        if kind == 2:
                            parts = [tile[k // ROWS].astype(jnp.float32) for k in (i, j)]
                            parts = [part[: ROWS // 2] * part[ROWS // 2 :] for part in parts]
                            made.append(jnp.concatenate(parts, axis=0).astype(jnp.bfloat16))
                            continue
                        one = jnp.broadcast_to(turned_ref[s + i : s + i + 1], (ROWS, LANES))
                        if kind == 1:
                            k = i + ROWS // 2
                            far = jnp.broadcast_to(turned_ref[s + k : s + k + 1], (ROWS, LANES))
                            near = (row >= i - j) & (row < i - j + ROWS // 2)
                            one = jnp.where(near, one, far)
                        made.append(one.astype(jnp.bfloat16) * tile[j // ROWS])
                    made += [nothing] * (per_chunk - len(made))
                    halves.append(jnp.concatenate(made, axis=0))
                pairs = jnp.concatenate(halves, axis=1)
                columns = slice(chunk * ROWS, chunk * ROWS + DEPTH)
                total += jnp.dot(fold_ref[:, columns], pairs, preferred_element_type=jnp.float32)
            rounded = total.astype(jnp.bfloat16).astype(jnp.float32)
            for half, s in enumerate(starts):
                kept = rounded[:chan, half * LANES : (half + 1) * LANES]
                back_ref[s : s + chan] = jnp.where(cloudy, kept, 0.0)
        out_ref[rows, :] = advected + back_ref[...].T[:, :width]
        keep(block).start()
        return carry

    back_ref[...] = jnp.zeros_like(back_ref)
    blocks = size_x * size_y // LANES
    lax.fori_loop(0, blocks, collide, 0)

    def finish(block, carry):
        keep(block).wait()
        return carry

    lax.fori_loop(0, blocks, finish, 0)


def per_device(hydro, winds, cloud_mask, coal_kernel, block_mask):
    size_x, size_y, width = hydro.shape
    levels = winds.shape[2] // 2
    chan = width // levels
    sides = []
    for axis, dim in (("gx", 0), ("gy", 1)):
        kind = jnp.bfloat16 if dim == 0 else jnp.float32
        last, first, up, down = edges(hydro, axis, dim)
        wlast, wfirst, _, _ = edges(winds, axis, dim)
        sides.append(lax.ppermute(jnp.concatenate([last, wlast], axis=-1).astype(kind), axis, up))
        sides.append(lax.ppermute(jnp.concatenate([first, wfirst], axis=-1).astype(kind), axis, down))
    fold = folded_kernel(coal_kernel, block_mask, chan)
    onto = (jnp.arange(levels)[:, None] == jnp.arange(width)[None, :] // chan).astype(jnp.bfloat16)
    onto = jnp.concatenate([onto] * 3, axis=0)
    mask = cloud_mask.reshape(-1, 1, LANES)
    long = round_up(width, LANES)
    result = pl.pallas_call(
        lambda *refs: step_kernel(levels, chan, *refs),
        out_shape=jax.ShapeDtypeStruct((size_x * size_y, width), jnp.float32),
        in_specs=[pl.BlockSpec(memory_space=pl.ANY)] + [pl.BlockSpec(memory_space=pltpu.VMEM)] * 8,
        out_specs=pl.BlockSpec(memory_space=pl.ANY),
        scratch_shapes=[
            pltpu.VMEM((long, LANES), jnp.float32),
            pltpu.VMEM((long, LANES), jnp.float32),
            pltpu.VMEM((size_y, width), jnp.float32),
            pltpu.VMEM((size_y + 16, width), jnp.float32),
            pltpu.VMEM((size_y + 16, 2 * levels), jnp.float32),
            pltpu.VMEM((size_x, size_y, width), jnp.float32),
            pltpu.VMEM((size_x * size_y, width), jnp.float32),
            pltpu.SemaphoreType.DMA((size_x,)),
            pltpu.SemaphoreType.DMA((size_x * size_y // LANES,)),
        ],
        compiler_params=pltpu.CompilerParams(vmem_limit_bytes=56 * 2**20),
    )(hydro, winds, *sides, mask, onto, fold)
    return result.reshape(size_x, size_y, width)


def solution(mesh):
    in_specs = (P("gx", "gy", None), P("gx", "gy", None), P("gx", "gy"), P(), P())
    out_specs = P("gx", "gy", None)
    return jax.shard_map(
        per_device, mesh=mesh, in_specs=in_specs, out_specs=out_specs, check_vma=False
    )
```
